512 devices in a mesh: ctx: 32 (over z, core), tp: 4 (over x), dp: 4 (over y).
Axes of the slice: x: 4, y: 4, z: 16, core: 2. Of those that a mesh axis runs over, the one named last changes fastest.
Arguments:
- attention_out: bfloat16 [8192, 4096], P('ctx', ('tp', 'dp')), may hold values from -6 to 6
- output_weight: bfloat16 [4096, 2048], P(('tp', 'dp')), may hold values from -0.09375 to 0.09375
- residual: bfloat16 [8192, 2048], P(('ctx', 'tp')), may hold values from -6 to 6
- norm_gain: float32 [2048], replicated, may hold values from 0.25 to 1.75
- routed_experts: int32 [8192, 8], P(('ctx', 'tp')), may hold values from 0 to 127, as said below
- route_weights: float32 [8192, 8], P(('ctx', 'tp')), may hold values from 0.05 to 1
- gate_weight: bfloat16 [128, 1024, 2048], P(('ctx', 'tp'), 'dp'), may hold values from -0.125 to 0.125
- up_weight: bfloat16 [128, 1024, 2048], P(('ctx', 'tp'), 'dp'), may hold values from -0.125 to 0.125
- down_weight: bfloat16 [128, 1024, 2048], P(('ctx', 'tp'), 'dp'), may hold values from -0.75 to 0.75
Outputs:
- layer_out: bfloat16 [8192, 2048], P(('ctx', 'tp', 'dp'))
The draws below stay inside these ranges and needn't reach their ends.
Inputs may be any that keep to these rules, and one draw needn't show every extreme that they name: `routed_experts`: each row names 8 different experts. In each aligned block of 64 rows no expert is named by more than 8 rows, and one expert, the same for all blocks, is named by exactly 8 rows in every block.
All inputs are finite; a program needn't handle non-finite values.
Results may differ from the reference program's by a relative error of at most 0.009.
Values may be sent and summed in bfloat16 or wider, within the bound.
A program may use at most 64 MiB of HBM per device.

```python
import math
import jax
import jax.numpy as jnp
from jax import lax

D = 2048
HEADS = 32
HEAD_DIM = 128
FFE = 1024
TOP = 8
ROWS_DEV = 64
EXPERTS = 128
CAP = 8
TOKENS = 8192


def draw_routed_experts(key, part):
    block_count = TOKENS // ROWS_DEV
    pool_size = EXPERTS * CAP
    needed = ROWS_DEV * TOP
    base = jax.random.fold_in(key, 11)
    rank_key, block_key = jax.random.split(base)
    popularity = jax.random.permutation(rank_key, EXPERTS).astype(jnp.int32)
    copy_expert = jnp.repeat(jnp.arange(EXPERTS, dtype=jnp.int32), CAP)
    copy_rank = popularity[copy_expert]
    tier = 1 + copy_rank * 8 // EXPERTS
    position = jnp.arange(pool_size, dtype=jnp.int32)
    column = jnp.arange(TOP, dtype=jnp.int32)[None, :]

    def one_block(one_key):
        noise_key, order_key, column_key = jax.random.split(one_key, 3)
        noise = jax.random.randint(noise_key, (pool_size,), 0, 4096, dtype=jnp.int32)
        score = jnp.where(copy_rank == 0, -1, noise * tier)
        score = score * pool_size + position
        order = jnp.argsort(score, stable=True)
        chosen = copy_expert[order[:needed]]
        grouped = jnp.sort(chosen)
        grid = grouped.reshape(TOP, ROWS_DEV).T
        row_order = jax.random.permutation(order_key, ROWS_DEV)
        grid = grid[row_order]
        column_score = jax.random.randint(column_key, (ROWS_DEV, TOP), 0, 4096, dtype=jnp.int32) * TOP + column
        column_order = jnp.argsort(column_score, axis=1, stable=True)
        return jnp.take_along_axis(grid, column_order, axis=1)
    keys = jax.random.split(block_key, block_count)
    return jax.vmap(one_block)(keys).reshape(TOKENS, TOP).astype(jnp.int32)


def spiked(entries, stream_key, source, target, shards_of, factor):
    def block_of(axis_at):
        return (jnp.arange(entries.shape[axis_at]) // (entries.shape[axis_at] // shards_of)).reshape((-1,) + (1,) * (entries.ndim - 1 - axis_at))

    one_side = jax.random.permutation(stream_key, shards_of)[block_of(target)]
    other_side = (block_of(target) + shards_of // 2) % shards_of
    return jnp.where((block_of(source) == one_side) | (block_of(source) == other_side), factor * entries, entries)


def level_of(own_key, shape, shards, least, largest):
    factor_of = 1.0
    for dim, shards_of in shards:
        heights = jax.random.uniform(jax.random.fold_in(jax.random.fold_in(own_key, 6), dim), (shards_of,), jnp.float32, least / len(shards), largest / len(shards))
        factor_of = factor_of * jnp.repeat(jnp.exp(heights), shape[dim] // shards_of).reshape((-1,) + (1,) * (len(shape) - 1 - dim))
    return factor_of


def scatter_about(key, shape, spread, limit, cuts=(), held_as=jnp.bfloat16):
    gain = level_of(key, shape, cuts, -0.22, 0.18) if cuts else 1.0
    values = jax.random.normal(key, shape, jnp.float32) * spread * gain
    return jnp.minimum(jnp.maximum(values, -limit), limit).astype(held_as)


def noise_with(rng, dims, deviation, limit, shards, heavy, kind=jnp.bfloat16):
    array = deviation * jax.random.normal(rng, dims, jnp.float32)
    if shards:
        array = array * level_of(rng, dims, shards, -0.22, 0.18)
    return jnp.clip(spiked(array, jax.random.fold_in(rng, 3), *heavy), -limit, limit).astype(kind)


def setup_inputs(seed: int = 0) -> dict:
    key_of = jax.random.split(jax.random.key(seed), 10)
    attention_out = noise_with(key_of[0], (TOKENS, HEADS * HEAD_DIM), 1.0, 6.0, ((0, 32), (1, 16)), (1, 0, 32, 2.75))
    output_weight = scatter_about(key_of[1], (HEADS * HEAD_DIM, D), (HEADS * HEAD_DIM) ** -0.5, 0.09375, ((0, 16),))
    residual = scatter_about(key_of[2], (TOKENS, D), 1.0, 6.0, ((0, 128),))
    norm_gain = jnp.clip(1.0 + 0.15 * jax.random.normal(key_of[3], (D,), jnp.float32), 0.25, 1.75)
    routed_experts = draw_routed_experts(jax.random.fold_in(key_of[9], 71), 0)
    route_weights = jnp.clip(jnp.exp(math.log(1.0) - 2.9957323 * jax.random.uniform(key_of[5], (TOKENS, TOP), jnp.float32) ** level_of(key_of[5], (TOKENS, TOP), ((0, 128),), -0.2, 0.2)), 0.05, 1.0)
    gate_weight = scatter_about(key_of[6], (EXPERTS, FFE, D), D ** -0.5, 0.125, ((0, 128), (1, 4)))
    up_weight = scatter_about(key_of[7], (EXPERTS, FFE, D), D ** -0.5, 0.125, ((0, 128), (1, 4)))
    down_weight = scatter_about(key_of[8], (EXPERTS, FFE, D), (FFE // 16) ** -0.5, 0.75, ((0, 128), (1, 4)))
    return {"attention_out": attention_out, "output_weight": output_weight, "residual": residual, "norm_gain": norm_gain, "routed_experts": routed_experts, "route_weights": route_weights, "gate_weight": gate_weight, "up_weight": up_weight, "down_weight": down_weight}


def reference(attention_out, output_weight, residual, norm_gain, routed_experts, route_weights, gate_weight, up_weight, down_weight):
    projected = jnp.dot(attention_out, output_weight, preferred_element_type=jnp.float32)
    hidden_state = residual.astype(jnp.float32) + projected
    square = lax.optimization_barrier(jnp.mean(hidden_state * hidden_state, axis=-1, keepdims=True))
    normed = (hidden_state * lax.rsqrt(square + 1e-06) * norm_gain).astype(jnp.bfloat16)
    route_probs = route_weights / lax.optimization_barrier(jnp.sum(route_weights, axis=-1, keepdims=True))
    flat_ids = routed_experts.reshape(-1).astype(jnp.int32)
    flat_probs = route_probs.reshape(-1)
    flat_rows = (jnp.arange(TOKENS * TOP, dtype=jnp.int32) // TOP).astype(jnp.int32)
    slot_count = TOKENS // ROWS_DEV * CAP

    def serve(running, expert_item):
        expert_index, gate_matrix, up_matrix, down_matrix = expert_item
        matching = flat_ids == expert_index
        picked = jnp.nonzero(matching, size=slot_count, fill_value=0)[0].astype(jnp.int32)
        is_live = jnp.arange(slot_count, dtype=jnp.int32) < jnp.sum(matching.astype(jnp.int32))
        token_rows = flat_rows[picked]
        inputs = normed[token_rows]
        gate_act = lax.dot_general(inputs, gate_matrix, (((1,), (1,)), ((), ())), preferred_element_type=jnp.float32)
        up_act = lax.dot_general(inputs, up_matrix, (((1,), (1,)), ((), ())), preferred_element_type=jnp.float32)
        hidden = (jax.nn.silu(gate_act) * up_act).astype(jnp.bfloat16)
        output = jnp.dot(hidden, down_matrix, preferred_element_type=jnp.float32)
        weight = jnp.where(is_live, flat_probs[picked], 0.0)
        return (running.at[token_rows].add(output * weight[:, None]), None)
    start = jnp.zeros((TOKENS, D), jnp.float32)
    routed, _ = lax.scan(serve, start, (jnp.arange(EXPERTS, dtype=jnp.int32), gate_weight, up_weight, down_weight))
    return (hidden_state + routed).astype(jnp.bfloat16)
```

```python
import jax
import jax.numpy as jnp
from jax import lax
from jax.sharding import PartitionSpec as P

EPSILON = 1e-06
F32 = jnp.float32
BF16 = jnp.bfloat16


def on_device(
    attention_out,
    output_weight,
    residual,
    norm_gain,
    routed_experts,
    route_weights,
    gate_weight,
    up_weight,
    down_weight,
):
    rows, width = residual.shape
    top = routed_experts.shape[1]
    replicas = lax.axis_size("dp")
    quarter = rows // replicas
    replica = lax.axis_index("dp")
    experts = lax.axis_size("ctx") * lax.axis_size("tp")
    capacity = min(rows, 2 * rows * top // experts)
    share = capacity // replicas
    down_full = lax.all_gather(down_weight[0], "dp", axis=0, tiled=True)

    partial = jnp.dot(attention_out, output_weight, preferred_element_type=F32).astype(BF16)
    arrived = lax.all_to_all(
        partial.reshape(-1, quarter, width), ("tp", "dp"), split_axis=0, concat_axis=0, tiled=True
    )
    summed = jnp.sum(arrived.astype(F32), axis=0)
    own_residual = lax.dynamic_slice_in_dim(residual, replica * quarter, quarter, 0)
    own_state = own_residual.astype(F32) + summed
    square = jnp.mean(own_state * own_state, axis=-1, keepdims=True)
    own_normed = (own_state * lax.rsqrt(square + EPSILON) * norm_gain).astype(BF16)
    normed = lax.all_gather(own_normed, "dp", axis=0, tiled=True)

    flat_ids = routed_experts.reshape(-1)
    copies = flat_ids.shape[0]
    after = lax.broadcasted_iota(jnp.int32, (copies, copies), 0) > lax.broadcasted_iota(
        jnp.int32, (copies, copies), 1
    )
    before = jnp.sum(((flat_ids[:, None] == flat_ids[None, :]) & after).astype(jnp.int32), axis=1)
    local = before - replica * share
    wanted = jnp.where((local >= 0) & (local < share), flat_ids * share + local, -1)
    wanted = wanted.reshape(rows, top)
    slots = jnp.arange(experts * share, dtype=jnp.int32)
    match = wanted[:, :, None] == slots[None, None, :]
    pick = jnp.any(match, axis=1).astype(BF16)
    outgoing = lax.dot_general(pick, normed, (((0,), (0,)), ((), ())), preferred_element_type=F32)
    outgoing = outgoing.astype(BF16).reshape(experts, share, width)
    incoming = lax.all_to_all(outgoing, ("ctx", "tp"), split_axis=0, concat_axis=0, tiled=True)
    flat_rows = lax.all_gather(incoming.reshape(-1, width), "dp", axis=0, tiled=True)
    gate_act = lax.dot_general(
        flat_rows, gate_weight[0], (((1,), (1,)), ((), ())), preferred_element_type=F32
    )
    up_act = lax.dot_general(
        flat_rows, up_weight[0], (((1,), (1,)), ((), ())), preferred_element_type=F32
    )
    hidden = (jax.nn.silu(gate_act) * up_act).astype(BF16)
    hidden = lax.all_to_all(
        hidden.reshape(replicas, experts * share, -1), "dp", split_axis=0, concat_axis=0, tiled=True
    )
    hidden = jnp.moveaxis(hidden, 0, 1).reshape(experts * share, -1)
    result = jnp.dot(hidden, down_full, preferred_element_type=F32).astype(BF16)
    returned = lax.all_to_all(
        result.reshape(experts, share, width), ("ctx", "tp"), split_axis=0, concat_axis=0, tiled=True
    ).reshape(experts * share, width)
    probs = route_weights / jnp.sum(route_weights, axis=1, keepdims=True)
    spread = jnp.sum(jnp.where(match, probs[:, :, None], 0.0), axis=1)
    high = spread.astype(BF16)
    low = (spread - high.astype(F32)).astype(BF16)
    mixed = jnp.dot(high, returned, preferred_element_type=F32) + jnp.dot(
        low, returned, preferred_element_type=F32
    )
    pieces = mixed.astype(BF16).reshape(replicas, quarter, width)
    pieces = lax.all_to_all(pieces, "dp", 0, 0, tiled=True)
    return (own_state + jnp.sum(pieces.astype(F32), axis=0)).astype(BF16)


def solution(mesh):
    in_specs = (
        P("ctx", ("tp", "dp")),
        P(("tp", "dp"), None),
        P(("ctx", "tp"), None),
        P(),
        P(("ctx", "tp"), None),
        P(("ctx", "tp"), None),
        P(("ctx", "tp"), "dp", None),
        P(("ctx", "tp"), "dp", None),
        P(("ctx", "tp"), "dp", None),
    )
    out_specs = P(("ctx", "tp", "dp"), None)
    return jax.shard_map(
        on_device, mesh=mesh, in_specs=in_specs, out_specs=out_specs, check_vma=False
    )
```

```python
import functools
import jax
import jax.numpy as jnp
from jax import lax
from jax.experimental import pallas as pl
from jax.experimental.pallas import tpu as pltpu
from jax.sharding import PartitionSpec as P

EPSILON = 1e-06
F32 = jnp.float32
BF16 = jnp.bfloat16
MESH = pl.DeviceIdType.MESH
CAP = 8
CORES = 2
CHUNKS = 4
NT = (((1,), (1,)), ((), ()))


def kernel(
    size,
    attn_ref,
    weight_ref,
    residual_ref,
    gain_ref,
    ids_ref,
    choice_ref,
    gate_ref,
    up_ref,
    down_ref,
    out_ref,
    gate_v,
    up_v,
    down_v,
    part0,
    part1,
    first0,
    first1,
    sum0,
    sum1,
    last0,
    last1,
    state,
    normed,
    tokens,
    meta,
    mix,
    packed,
    gathered,
    hidden_out,
    hidden,
    answers,
    returned,
    partial,
    chain_in,
    chain_out,
    final,
    finished,
    local_sem,
    a0s, a0r, a1s, a1r, b0s, b0r, b1s, b1r,
    ns, nr,
    ds, dr,
    zs, zr, ms, mr,
    xs, xr,
    ys, yr,
    hs, hr,
    rs, rr,
    qs, qr,
    fs, fr,
):
    nz, nc, nx, ny = size
    units = nc * nx
    turns = nz // ny
    half_ring = nz // 2
    ctx, x, y = lax.axis_index("ctx"), lax.axis_index("tp"), lax.axis_index("dp")
    z, c = lax.div(ctx, nc), lax.rem(ctx, nc)
    me = c * nx + x
    own, width = out_ref.shape
    rows = own * ny
    half = width // 2
    share = gate_v.shape[0]
    block = 2 * rows
    piece = block // CHUNKS
    unit = 2 * CAP
    sends = []

    def remote(src, dst, send_sem, recv_sem, device):
        return pltpu.make_async_remote_copy(
            src_ref=src, dst_ref=dst, send_sem=send_sem, recv_sem=recv_sem,
            device_id=device, device_id_type=MESH,
        )

    def send(src, dst, send_sem, recv_sem, device, when=None):
        copy = remote(src, dst, send_sem, recv_sem, device)
        if when is None:
            copy.start()
        else:
            @pl.when(when)
            def _():
                copy.start()
        sends.append((when, copy))

    def arrived(dst, recv_sem):
        remote(dst, dst, local_sem.at[3], recv_sem, ahead).wait_recv()

    def y_of(step):
        return lax.rem(y + step, ny)

    ahead = (lax.rem(z + 1, nz) * nc + c, x, y)
    behind = (lax.rem(z + nz - 1, nz) * nc + c, x, y)
    x_steps = [(0, dx) for dx in range(1, nx)]
    plane_steps = [(dc, dx) for dc in range(nc) for dx in range(nx) if (dc, dx) != (0, 0)]

    def plane_peer(step):
        pc, px = lax.rem(c + step[0], nc), lax.rem(x + step[1], nx)
        return pc * nx + px, (z * nc + pc, px, y)

    peers = [ahead, behind]
    peers += [plane_peer(s)[1] for s in plane_steps]
    peers += [(ctx, x, y_of(s)) for s in range(1, ny)]
    barrier = pltpu.get_barrier_semaphore()
    for peer in peers:
        pl.semaphore_signal(barrier, inc=1, device_id=peer, device_id_type=MESH)

    def down_rows(at_y, part=0, parts=1):
        count = share // parts
        return down_v.at[pl.ds(pl.multiple_of(at_y * share + part * count, count), count)]

    local = [
        pltpu.make_async_copy(gate_ref, gate_v, local_sem.at[0]),
        pltpu.make_async_copy(up_ref, up_v, local_sem.at[1]),
        pltpu.make_async_copy(down_ref, down_rows(y), local_sem.at[2]),
    ]
    for copy in (local[2], local[0], local[1]):
        copy.start()

    attn = attn_ref[...]
    cols = half // 2
    for j in range(2):
        at = pl.ds(j * cols, cols)
        prod = jnp.dot(attn, weight_ref[:, at], preferred_element_type=F32).astype(BF16)
        for px in range(nx):
            for py in range(ny):
                lo = px * rows + py * own
                part0[py, px, :, at] = prod[lo : lo + own]
    pl.semaphore_wait(barrier, len(peers))
    for s in range(1, ny):
        py = y_of(s)
        send(part0.at[py], first0.at[y], a0s.at[py], a0r.at[y], (ctx, x, py))
    for j in range(2):
        at = pl.ds(j * cols, cols)
        prod = jnp.dot(
            attn, weight_ref[:, pl.ds(half + j * cols, cols)], preferred_element_type=F32
        ).astype(BF16)
        for px in range(nx):
            for py in range(ny):
                lo = px * rows + py * own
                part1[px, py, :, at] = prod[lo : lo + own]
    for s in x_steps:
        px = lax.rem(x + s[1], nx)
        send(part1.at[px], first1.at[x], a1s.at[px], a1r.at[x], (ctx, px, y))

    ids = ids_ref[...].astype(F32)
    top = ids.shape[0]
    experts = nz * units
    expert_row = lax.broadcasted_iota(jnp.int32, (experts, block), 0).astype(F32)
    named = jnp.zeros((experts, block), F32)
    for k in range(top):
        named = jnp.where(ids[k : k + 1] == expert_row, 1.0, named)
    from_row = lax.broadcasted_iota(jnp.int32, (block, block), 0)
    to_row = lax.broadcasted_iota(jnp.int32, (block, block), 1)
    earlier = jnp.where(
        jnp.logical_or(
            from_row < jnp.minimum(to_row, rows),
            jnp.logical_and(from_row < to_row - rows, from_row < rows),
        ),
        1.0,
        0.0,
    )
    earlier = jnp.where(
        jnp.logical_and(to_row >= rows, from_row >= to_row - rows), 0.0, earlier
    )
    count = jnp.dot(named.astype(BF16), earlier.astype(BF16), preferred_element_type=F32)
    slots = jnp.concatenate(
        [
            jnp.sum(jnp.where(ids[k : k + 1] == expert_row, count, 0.0), axis=0, keepdims=True)
            for k in range(top)
        ],
        axis=0,
    )
    choice = choice_ref[...]
    probs = choice / jnp.sum(choice, axis=0, keepdims=True)
    high = probs.astype(BF16).astype(F32)
    turn_own = lax.div(z, ny)
    y_own = lax.rem(z, ny)
    routing = jnp.concatenate([ids, slots, high, probs - high], axis=0).astype(BF16)
    is_owner = y == y_own

    @pl.when(is_owner)
    def _():
        meta[turn_own] = routing

    local[2].wait()
    for i, s in enumerate((1, ny - 1) if ny > 2 else (1,)):
        py = y_of(s)
        send(down_rows(y), down_rows(y), ds.at[i], dr.at[y, 0], (ctx, x, py))

    for s in range(1, ny):
        py = y_of(s)
        arrived(first0.at[py], a0r.at[py])
    for px in range(nx):
        total = part0[y, px].astype(F32)
        for s in range(1, ny):
            total += first0[y_of(s), px].astype(F32)
        sum0[px] = total.astype(BF16)
    for s in x_steps:
        px = lax.rem(x + s[1], nx)
        send(sum0.at[px], last0.at[x], b0s.at[px], b0r.at[x], (ctx, px, y))
    for s in x_steps:
        px = lax.rem(x + s[1], nx)
        arrived(first1.at[px], a1r.at[px])
    for py in range(ny):
        total = part1[x, py].astype(F32)
        for s in x_steps:
            total += first1[lax.rem(x + s[1], nx), py].astype(F32)
        sum1[py] = total.astype(BF16)
    for s in range(1, ny):
        py = y_of(s)
        send(sum1.at[py], last1.at[y], b1s.at[py], b1r.at[y], (ctx, x, py))
    mine = pl.ds(pl.multiple_of(y * own, own), own)
    low_sum = sum0[x].astype(F32) + residual_ref[mine, :half].astype(F32)
    high_sum = sum1[y].astype(F32) + residual_ref[mine, half:].astype(F32)
    for s in x_steps:
        px = lax.rem(x + s[1], nx)
        arrived(last0.at[px], b0r.at[px])
        low_sum += last0[px].astype(F32)
    for s in range(1, ny):
        py = y_of(s)
        arrived(last1.at[py], b1r.at[py])
        high_sum += last1[py].astype(F32)
    state[0] = low_sum
    state[1] = high_sum
    square = (
        jnp.sum(low_sum * low_sum, axis=-1, keepdims=True)
        + jnp.sum(high_sum * high_sum, axis=-1, keepdims=True)
    ) / width
    scale = lax.rsqrt(square + EPSILON)
    normed[0] = (low_sum * scale * gain_ref[:, :half]).astype(BF16)
    normed[1] = (high_sum * scale * gain_ref[:, half:]).astype(BF16)

    for h in range(2):
        place = pl.ds(pl.multiple_of(h * rows + y * own, own), own)
        send(
            normed.at[h], tokens.at[turn_own, place, :], ns.at[h], nr.at[y, h],
            (ctx, x, y_own), when=y != y_own,
        )

    @pl.when(is_owner)
    def _():
        for h in range(2):
            place = pl.ds(pl.multiple_of(h * rows + y * own, own), own)
            tokens[turn_own, place, :] = normed[h]
        for s in range(1, ny):
            py = y_of(s)
            for h in range(2):
                place = pl.ds(pl.multiple_of(h * rows + py * own, own), own)
                arrived(tokens.at[turn_own, place, :], nr.at[py, h])

    def turn(r, at_y):
        off = lax.rem(z + ny - at_y, ny)
        late = lax.div(2 * off, ny + 1)
        if turns == 4:
            near, far = ((0, 3), (3, 0), (1, 2), (2, 1))[r]
        elif turns == 2:
            near, far = ((0, 1), (1, 0))[r]
        else:
            near, far = 0, 0
        distance = off + ny * (near + (far - near) * late)
        return lax.div(lax.rem(z + nz - distance, nz), ny), distance

    my_turns = [turn(r, y) for r in range(turns)]

    def z_step(r, k):
        t, d = my_turns[r]
        at = pl.ds(k * piece, piece)
        ref, sem = tokens.at[t, at, :], zr.at[t, k]

        @pl.when(d > 0)
        def _():
            arrived(ref, sem)
            if k == 0:
                arrived(meta.at[t], mr.at[t])

        forward, backward = d < half_ring, jnp.logical_or(d == 0, d > half_ring + 1)
        for way, (go, device) in enumerate(((forward, ahead), (backward, behind))):
            send(ref, ref, zs.at[way, t, k], sem, device, when=go)
            if k == 0:
                send(meta.at[t], meta.at[t], ms.at[way, t], mr.at[t], device, when=go)

    slot_row = lax.broadcasted_iota(jnp.int32, (unit, block), 0)
    token_lane = lax.broadcasted_iota(jnp.int32, (unit, block), 1)
    same_half = lax.div(slot_row, CAP) == lax.div(token_lane, rows)
    slot_want = jnp.where(same_half, lax.rem(slot_row, CAP), -2).astype(F32)

    def pack(r):
        t, _ = my_turns[r]
        table = meta[t].astype(F32)
        first = (z * units).astype(F32)
        picks, highs, lows = [], [], []
        for u in range(units):
            got = jnp.full((unit, block), -1.0, F32)
            big = jnp.zeros((unit, block), F32)
            small = jnp.zeros((unit, block), F32)
            for k in range(top):
                hit = table[k : k + 1] == first + float(u)
                got = jnp.where(hit, table[top + k : top + k + 1], got)
                big = jnp.where(hit, table[2 * top + k : 2 * top + k + 1], big)
                small = jnp.where(hit, table[3 * top + k : 3 * top + k + 1], small)
            hit = got == slot_want
            picks.append(jnp.where(hit, 1.0, 0.0))
            highs.append(jnp.where(hit, big, 0.0))
            lows.append(jnp.where(hit, small, 0.0))
        chosen = jnp.concatenate(picks, axis=0).astype(BF16)
        mix[t, 0] = jnp.concatenate(highs, axis=0).T.astype(BF16)
        mix[t, 1] = jnp.concatenate(lows, axis=0).T.astype(BF16)
        for j in range(2):
            at = pl.ds(j * cols, cols)
            out = jnp.dot(chosen, tokens[t, :, at], preferred_element_type=F32)
            packed[t, :, :, at] = out.astype(BF16).reshape(units, unit, cols)
        for i, s in enumerate(plane_steps):
            index, device = plane_peer(s)
            send(
                packed.at[t, index], gathered.at[y, t, me], xs.at[t, i], xr.at[t, me], device
            )
        gathered[y, t, me] = packed[t, me]

    def y_send(r):
        t, _ = my_turns[r]
        for s in plane_steps:
            index, _ = plane_peer(s)
            arrived(gathered.at[y, t, index], xr.at[t, index])
        for i, s in enumerate((1, ny - 1) if ny > 2 else (1,)):
            send(
                gathered.at[y, t], gathered.at[y, t], ys.at[i, t], yr.at[y, t, 0],
                (ctx, x, y_of(s)),
            )

    def y_forward(r):
        for i, s in enumerate((ny - 1, 1) if ny > 2 else (1,)):
            py = y_of(s)
            t, _ = turn(r, py)
            arrived(gathered.at[py, t], yr.at[py, t, 0])
            if ny > 2:
                part = gathered.at[py, t, pl.ds(i * (units // 2), units // 2)]
                send(part, part, ys.at[2 + i, t], yr.at[py, t, 1 + i], (ctx, x, y_of(ny - s)))

    def y_last(r):
        if ny > 2:
            py = y_of(2)
            t, _ = turn(r, py)
            for i in range(2):
                part = gathered.at[py, t, pl.ds(i * (units // 2), units // 2)]
                arrived(part, yr.at[py, t, 1 + i])

    def d_forward():
        for i, s in enumerate((ny - 1, 1) if ny > 2 else (1,)):
            py = y_of(s)
            arrived(down_rows(py), dr.at[py, 0])
            if ny > 2:
                part = down_rows(py, i, 2)
                send(part, part, ds.at[2 + i], dr.at[py, 1 + i], (ctx, x, y_of(ny - s)))

    def d_last():
        if ny > 2:
            py = y_of(2)
            for i in range(2):
                part = down_rows(py, i, 2)
                arrived(part, dr.at[py, 1 + i])

    def expert(r, s):
        py = y_of(s)
        t, _ = turn(r, py)
        data = gathered[py, t].reshape(units * unit, half)

        def both(weights):
            low = lax.dot_general(data, weights[:, :half], NT, preferred_element_type=F32)
            high = lax.dot_general(data, weights[:, half:], NT, preferred_element_type=F32)
            low = low.reshape(units, unit, share)[:, :CAP]
            return low + high.reshape(units, unit, share)[:, CAP:]

        gate_act = both(gate_v)
        up_act = both(up_v)
        act = gate_act / (1.0 + jnp.exp(-gate_act)) * up_act
        act = act.reshape(units * CAP, share).astype(BF16)
        place = pl.ds(pl.multiple_of(y * share, share), share)
        if s == 0:
            hidden[t, :, place] = act
        else:
            hidden_out[s - 1, r] = act
            send(
                hidden_out.at[s - 1, r], hidden.at[t, :, place], hs.at[s - 1, r], hr.at[y, t],
                (ctx, x, py),
            )

    if turns == 4:
        for k in range(CHUNKS):
            z_step(0, k)
            z_step(1, k)
        pack(0)
        pack(1)
        for k in range(CHUNKS):
            z_step(2, k)
            z_step(3, k)
            if k == 1:
                y_send(0)
        y_send(1)
        pack(2)
        pack(3)
        d_forward()
        y_forward(0)
        y_send(2)
        local[0].wait()
        local[1].wait()
        expert(0, 0)
        y_forward(1)
        y_send(3)
        expert(1, 0)
        expert(0, 1)
        expert(0, 3)
        y_last(0)
        expert(0, 2)
        y_forward(2)
        expert(1, 1)
        expert(1, 3)
        expert(2, 0)
        y_last(1)
        expert(1, 2)
        y_forward(3)
        expert(3, 0)
        expert(2, 1)
        expert(2, 3)
        y_last(2)
        expert(2, 2)
        expert(3, 1)
        expert(3, 3)
        y_last(3)
        expert(3, 2)
    else:
        for k in range(CHUNKS):
            for r in range(turns):
                z_step(r, k)
        for r in range(turns):
            pack(r)
        d_forward()
        local[0].wait()
        local[1].wait()
        for r in range(turns):
            y_send(r)
        for r in range(turns):
            y_forward(r)
        for r in range(turns):
            y_last(r)
            for s in range(ny):
                expert(r, s)
    d_last()

    def answer(r):
        t, _ = my_turns[r]
        for s in range(1, ny):
            py = y_of(s)
            arrived(hidden.at[t, :, pl.ds(pl.multiple_of(py * share, share), share)], hr.at[py, t])
        data = hidden[t]
        step = half // 4
        for j in range(4):
            low = jnp.dot(data, down_v[:, pl.ds(j * step, step)], preferred_element_type=F32)
            high = jnp.dot(data, down_v[:, pl.ds(half + j * step, step)], preferred_element_type=F32)
            low = low.reshape(units, CAP, step)
            high = high.reshape(units, CAP, step)
            both = jnp.concatenate([low, high], axis=1)
            answers[t, :, :, pl.ds(j * step, step)] = both.astype(BF16)
        for i, s in enumerate(plane_steps):
            index, device = plane_peer(s)
            send(answers.at[t, index], returned.at[t, me], rs.at[t, i], rr.at[t, me], device)
        returned[t, me] = answers[t, me]

    def combine(r):
        t, _ = my_turns[r]
        for s in plane_steps:
            index, _ = plane_peer(s)
            arrived(returned.at[t, index], rr.at[t, index])
        for j in range(2):
            at = pl.ds(j * cols, cols)
            data = returned[t, :, :, at].reshape(units * unit, cols)
            partial[t, :, at] = jnp.dot(
                mix[t, 0], data, preferred_element_type=F32
            ) + jnp.dot(mix[t, 1], data, preferred_element_type=F32)

    def z_reduce(r, k):
        t, d = my_turns[r]
        at = pl.ds(k * piece, piece)
        onward = lax.div(d, half_ring + 1)
        next_z = lax.rem(z + nz + 2 * onward - 1, nz)
        slot = t + (turns - t) * lax.div(d, nz - 1)
        starts = jnp.logical_or(d == half_ring, d == half_ring + 1)

        @pl.when(starts)
        def _():
            chain_out[t, at, :] = partial[t, at, :].astype(BF16)

        @pl.when(jnp.logical_not(starts))
        def _():
            arrived(chain_in.at[t, at, :], qr.at[t, k])
            total = partial[t, at, :] + chain_in[t, at, :].astype(F32)
            if r < 2:
                partial[t, at, :] = total
            chain_out[t, at, :] = total.astype(BF16)

        send(
            chain_out.at[t, at, :], chain_in.at[slot, at, :], qs.at[t, k], qr.at[slot, k],
            (next_z * nc + c, x, y), when=d > 0,
        )
        if r < 2:
            @pl.when(d == 0)
            def _():
                arrived(chain_in.at[turns, at, :], qr.at[turns, k])
                total = partial[t, at, :] + chain_in[turns, at, :].astype(F32)
                final[at, :] = total.astype(BF16)

    def hand_out():
        for h in range(2):
            for py in range(ny):
                place = pl.ds(h * rows + py * own, own)
                send(
                    final.at[place, :], finished.at[h], fs.at[h, py], fr.at[h], (ctx, x, py),
                    when=jnp.logical_and(is_owner, y != py),
                )

    if turns == 4:
        for r in (3, 2, 1, 0):
            answer(r)
        combine(3)
        combine(2)
        for k in range(CHUNKS):
            z_reduce(3, k)
            z_reduce(2, k)
            if k == 0:
                combine(1)
                combine(0)
        for k in range(CHUNKS):
            z_reduce(1, k)
            z_reduce(0, k)
    else:
        for r in range(turns - 1, -1, -1):
            answer(r)
        for r in range(turns - 1, -1, -1):
            combine(r)
        for k in range(CHUNKS):
            for r in range(turns - 1, -1, -1):
                z_reduce(r, k)
    hand_out()

    @pl.when(is_owner)
    def _():
        for h in range(2):
            place = pl.ds(pl.multiple_of(h * rows + y * own, own), own)
            finished[h] = final[place, :]

    @pl.when(jnp.logical_not(is_owner))
    def _():
        for h in range(2):
            arrived(finished.at[h], fr.at[h])

    for h in range(2):
        out_ref[:, pl.ds(h * half, half)] = (state[h] + finished[h].astype(F32)).astype(BF16)

    for when, copy in sends:
        if when is None:
            copy.wait_send()
        else:
            @pl.when(when)
            def _():
                copy.wait_send()


def on_device(
    size,
    attention_out,
    output_weight,
    residual,
    norm_gain,
    routed_experts,
    route_weights,
    gate_weight,
    up_weight,
    down_weight,
):
    nz, nc, nx, ny = size
    rows, width = residual.shape
    own, half = rows // ny, width // 2
    share = gate_weight.shape[1]
    top = routed_experts.shape[1]
    units, turns, unit, block = nc * nx, nz // ny, 2 * CAP, 2 * rows
    ids = jnp.concatenate([routed_experts.T, routed_experts.T], axis=1)
    choice = jnp.concatenate([route_weights.T, route_weights.T], axis=1)

    def vmem(*shape, dtype=BF16):
        return pltpu.VMEM(shape, dtype)

    def sems(*shape):
        return pltpu.SemaphoreType.DMA(shape)

    whole = pl.BlockSpec(memory_space=pltpu.VMEM)
    far = pl.BlockSpec(memory_space=pl.ANY)
    return pl.pallas_call(
        functools.partial(kernel, size),
        out_shape=jax.ShapeDtypeStruct((own, width), BF16),
        in_specs=[whole] * 6 + [far] * 3,
        out_specs=whole,
        scratch_shapes=[
            vmem(share, width),
            vmem(share, width),
            vmem(ny * share, width),
            vmem(ny, nx, own, half),
            vmem(nx, ny, own, half),
            vmem(ny, nx, own, half),
            vmem(nx, ny, own, half),
            vmem(nx, own, half),
            vmem(ny, own, half),
            vmem(nx, own, half),
            vmem(ny, own, half),
            vmem(2, own, half, dtype=F32),
            vmem(2, own, half),
            vmem(turns, block, half),
            vmem(turns, 4 * top, block),
            vmem(turns, 2, block, units * unit),
            vmem(turns, units, unit, half),
            vmem(ny, turns, units, unit, half),
            vmem(ny - 1, turns, units * CAP, share),
            vmem(turns, units * CAP, ny * share),
            vmem(turns, units, unit, half),
            vmem(turns, units, unit, half),
            vmem(turns, block, half, dtype=F32),
            vmem(turns + 1, block, half),
            vmem(turns, block, half),
            vmem(block, half),
            vmem(2, own, half),
            sems(4),
            sems(ny), sems(ny), sems(nx), sems(nx), sems(nx), sems(nx), sems(ny), sems(ny),
            sems(2), sems(ny, 2),
            sems(4), sems(ny, 3),
            sems(2, turns, CHUNKS), sems(turns, CHUNKS), sems(2, turns), sems(turns),
            sems(turns, units), sems(turns, units),
            sems(4, turns), sems(ny, turns, 3),
            sems(ny, turns), sems(ny, turns),
            sems(turns, units), sems(turns, units),
            sems(turns, CHUNKS), sems(turns + 1, CHUNKS),
            sems(2, ny), sems(2),
        ],
        compiler_params=pltpu.CompilerParams(
            collective_id=0, has_side_effects=True, vmem_limit_bytes=56 * 1024 * 1024
        ),
    )(
        attention_out, output_weight, residual, norm_gain.reshape(1, -1), ids, choice,
        gate_weight[0], up_weight[0], down_weight[0],
    )


def solution(mesh):
    nc = min(CORES, mesh.shape["ctx"])
    size = (mesh.shape["ctx"] // nc, nc, mesh.shape["tp"], mesh.shape["dp"])
    in_specs = (
        P("ctx", ("tp", "dp")),
        P(("tp", "dp"), None),
        P(("ctx", "tp"), None),
        P(),
        P(("ctx", "tp"), None),
        P(("ctx", "tp"), None),
        P(("ctx", "tp"), "dp", None),
        P(("ctx", "tp"), "dp", None),
        P(("ctx", "tp"), "dp", None),
    )
    out_specs = P(("ctx", "tp", "dp"), None)
    return jax.shard_map(
        functools.partial(on_device, size),
        mesh=mesh, in_specs=in_specs, out_specs=out_specs, check_vma=False,
    )
```

```python
import functools
import jax
import jax.numpy as jnp
from jax import lax
from jax.experimental import pallas as pl
from jax.experimental.pallas import tpu as pltpu
from jax.sharding import PartitionSpec as P

EPSILON = 1e-06
F32 = jnp.float32
BF16 = jnp.bfloat16
MESH = pl.DeviceIdType.MESH
CAP = 8
CORES = 2
CHUNKS = 4
HOP = 3
NT = (((1,), (1,)), ((), ()))


def kernel(
    size,
    attn_ref,
    weight_ref,
    residual_ref,
    gain_ref,
    ids_ref,
    choice_ref,
    gate_ref,
    up_ref,
    down_ref,
    out_ref,
    gate_v,
    up_v,
    down_v,
    part0,
    part1,
    first0,
    first1,
    sum0,
    sum1,
    last0,
    last1,
    state,
    normed,
    tokens,
    meta,
    mix,
    packed,
    gathered,
    hidden_out,
    hidden,
    answers,
    returned,
    partial,
    chain_in,
    chain_out,
    final,
    finished,
    local_sem,
    a0s, a0r, a1s, a1r, b0s, b0r, b1s, b1r,
    ns, nr,
    ds, dr,
    zs, zr, ms, mr,
    xs, xr,
    ys, yr,
    hs, hr,
    rs, rr,
    qs, qr,
    fs, fr,
):
    nz, nc, nx, ny = size
    units = nc * nx
    turns = nz // ny
    half_ring = nz // 2
    ctx, x, y = lax.axis_index("ctx"), lax.axis_index("tp"), lax.axis_index("dp")
    z, c = lax.div(ctx, nc), lax.rem(ctx, nc)
    me = c * nx + x
    own, width = out_ref.shape
    rows = own * ny
    half = width // 2
    share = gate_v.shape[0]
    block = 2 * rows
    piece = block // CHUNKS
    unit = 2 * CAP
    sends = []

    def remote(src, dst, send_sem, recv_sem, device):
        return pltpu.make_async_remote_copy(
            src_ref=src, dst_ref=dst, send_sem=send_sem, recv_sem=recv_sem,
            device_id=device, device_id_type=MESH,
        )

    def send(src, dst, send_sem, recv_sem, device, when=None):
        copy = remote(src, dst, send_sem, recv_sem, device)
        if when is None:
            copy.start()
        else:
            @pl.when(when)
            def _():
                copy.start()
        sends.append((when, copy))

    def arrived(dst, recv_sem):
        remote(dst, dst, local_sem.at[3], recv_sem, ahead).wait_recv()

    def y_of(step):
        return lax.rem(y + step, ny)

    ahead = (lax.rem(z + 1, nz) * nc + c, x, y)
    behind = (lax.rem(z + nz - 1, nz) * nc + c, x, y)
    x_steps = [(0, dx) for dx in range(1, nx)]
    plane_steps = [(dc, dx) for dc in range(nc) for dx in range(nx) if (dc, dx) != (0, 0)]

    def plane_peer(step):
        pc, px = lax.rem(c + step[0], nc), lax.rem(x + step[1], nx)
        return pc * nx + px, (z * nc + pc, px, y)

    peers = [ahead, behind]
    peers += [plane_peer(s)[1] for s in plane_steps]
    peers += [(ctx, x, y_of(s)) for s in range(1, ny)]
    barrier = pltpu.get_barrier_semaphore()
    for peer in peers:
        pl.semaphore_signal(barrier, inc=1, device_id=peer, device_id_type=MESH)

    def down_rows(at_y, part=0, parts=1):
        count = share // parts
        return down_v.at[pl.ds(pl.multiple_of(at_y * share + part * count, count), count)]

    local = [
        pltpu.make_async_copy(gate_ref, gate_v, local_sem.at[0]),
        pltpu.make_async_copy(up_ref, up_v, local_sem.at[1]),
        pltpu.make_async_copy(down_ref, down_rows(y), local_sem.at[2]),
    ]
    for copy in (local[2], local[0], local[1]):
        copy.start()

    attn = attn_ref[...]
    cols = half // 2
    for j in range(2):
        at = pl.ds(j * cols, cols)
        prod = jnp.dot(attn, weight_ref[:, at], preferred_element_type=F32).astype(BF16)
        for px in range(nx):
            for py in range(ny):
                lo = px * rows + py * own
                part0[py, px, :, at] = prod[lo : lo + own]
    pl.semaphore_wait(barrier, len(peers))
    for s in range(1, ny):
        py = y_of(s)
        send(part0.at[py], first0.at[y], a0s.at[py], a0r.at[y], (ctx, x, py))
    for j in range(2):
        at = pl.ds(j * cols, cols)
        prod = jnp.dot(
            attn, weight_ref[:, pl.ds(half + j * cols, cols)], preferred_element_type=F32
        ).astype(BF16)
        for px in range(nx):
            for py in range(ny):
                lo = px * rows + py * own
                part1[px, py, :, at] = prod[lo : lo + own]
    for s in x_steps:
        px = lax.rem(x + s[1], nx)
        send(part1.at[px], first1.at[x], a1s.at[px], a1r.at[x], (ctx, px, y))

    def d_send(second):
        for i, s in enumerate((1, ny - 1) if ny > 2 else (1,)):
            j = 1 - i if second else i
            part = down_rows(y, j, 2)
            send(part, part, ds.at[2 * i + j], dr.at[y, j], (ctx, x, y_of(s)))

    ids = ids_ref[...].astype(F32)
    top = ids.shape[0]
    experts = nz * units
    expert_row = lax.broadcasted_iota(jnp.int32, (experts, block), 0).astype(F32)
    named = jnp.zeros((experts, block), F32)
    for k in range(top):
        named = jnp.where(ids[k : k + 1] == expert_row, 1.0, named)
    from_row = lax.broadcasted_iota(jnp.int32, (block, block), 0)
    to_row = lax.broadcasted_iota(jnp.int32, (block, block), 1)
    earlier = jnp.where(
        jnp.logical_or(
            from_row < jnp.minimum(to_row, rows),
            jnp.logical_and(from_row < to_row - rows, from_row < rows),
        ),
        1.0,
        0.0,
    )
    earlier = jnp.where(
        jnp.logical_and(to_row >= rows, from_row >= to_row - rows), 0.0, earlier
    )
    count = jnp.dot(named.astype(BF16), earlier.astype(BF16), preferred_element_type=F32)
    slots = jnp.concatenate(
        [
            jnp.sum(jnp.where(ids[k : k + 1] == expert_row, count, 0.0), axis=0, keepdims=True)
            for k in range(top)
        ],
        axis=0,
    )
    choice = choice_ref[...]
    probs = choice / jnp.sum(choice, axis=0, keepdims=True)
    high = probs.astype(BF16).astype(F32)
    turn_own = lax.div(z, ny)
    y_own = lax.rem(z, ny)
    routing = jnp.concatenate([ids, slots, high, probs - high], axis=0).astype(BF16)
    is_owner = y == y_own

    @pl.when(is_owner)
    def _():
        meta[turn_own] = routing

    for s in range(1, ny):
        py = y_of(s)
        arrived(first0.at[py], a0r.at[py])
    for px in range(nx):
        total = part0[y, px].astype(F32)
        for s in range(1, ny):
            total += first0[y_of(s), px].astype(F32)
        sum0[px] = total.astype(BF16)
    for s in x_steps:
        px = lax.rem(x + s[1], nx)
        send(sum0.at[px], last0.at[x], b0s.at[px], b0r.at[x], (ctx, px, y))
    for s in x_steps:
        px = lax.rem(x + s[1], nx)
        arrived(first1.at[px], a1r.at[px])
    for py in range(ny):
        total = part1[x, py].astype(F32)
        for s in x_steps:
            total += first1[lax.rem(x + s[1], nx), py].astype(F32)
        sum1[py] = total.astype(BF16)
    for s in range(1, ny):
        py = y_of(s)
        send(sum1.at[py], last1.at[y], b1s.at[py], b1r.at[y], (ctx, x, py))
    mine = pl.ds(pl.multiple_of(y * own, own), own)
    low_sum = sum0[x].astype(F32) + residual_ref[mine, :half].astype(F32)
    high_sum = sum1[y].astype(F32) + residual_ref[mine, half:].astype(F32)
    for s in x_steps:
        px = lax.rem(x + s[1], nx)
        arrived(last0.at[px], b0r.at[px])
        low_sum += last0[px].astype(F32)
    for s in range(1, ny):
        py = y_of(s)
        arrived(last1.at[py], b1r.at[py])
        high_sum += last1[py].astype(F32)
    state[0] = low_sum
    state[1] = high_sum
    square = (
        jnp.sum(low_sum * low_sum, axis=-1, keepdims=True)
        + jnp.sum(high_sum * high_sum, axis=-1, keepdims=True)
    ) / width
    scale = lax.rsqrt(square + EPSILON)
    normed[0] = (low_sum * scale * gain_ref[:, :half]).astype(BF16)
    normed[1] = (high_sum * scale * gain_ref[:, half:]).astype(BF16)

    for h in range(2):
        place = pl.ds(pl.multiple_of(h * rows + y * own, own), own)
        send(
            normed.at[h], tokens.at[turn_own, place, :], ns.at[h], nr.at[y, h],
            (ctx, x, y_own), when=y != y_own,
        )

    @pl.when(is_owner)
    def _():
        for h in range(2):
            place = pl.ds(pl.multiple_of(h * rows + y * own, own), own)
            tokens[turn_own, place, :] = normed[h]
        for s in range(1, ny):
            py = y_of(s)
            for h in range(2):
                place = pl.ds(pl.multiple_of(h * rows + py * own, own), own)
                arrived(tokens.at[turn_own, place, :], nr.at[py, h])

    local[2].wait()
    d_send(False)
    d_send(True)

    tables = {4: ((0, 3, 1, 2), (3, 0, 2, 1)), 2: ((0, 1), (1, 0)), 1: ((0,), (0,))}[turns]

    def turn(r, at_y):
        off = lax.rem(z + ny - at_y, ny)
        near, far = tables[0][r], tables[1][r]
        late = lax.div(2 * off, ny + 1)
        distance = off + ny * (near + (far - near) * late)
        return lax.div(lax.rem(z + nz - distance, nz), ny), distance

    my_turns = [turn(r, y) for r in range(turns)]
    my_off = lax.rem(z + ny - y, ny)

    def hops_at(off, r):
        return off + ny * tables[2 * off // (ny + 1)][r]

    def steps_out(off):
        order = []
        for r in range(turns):
            d = hops_at(off, r)
            order += [(HOP * min(d, nz - d) + k, r, k) for k in range(CHUNKS)]
        return sorted(order)

    def steps_back(off):
        order = []
        for r in range(turns):
            d = hops_at(off, r)
            waited = half_ring - d if d <= half_ring else d - half_ring - 1
            order += [(HOP * waited + k, r, k) for k in range(CHUNKS)]
        return sorted(order)

    def for_offset(run):
        for off in range(ny):
            @pl.when(my_off == off)
            def _():
                run(off)

    def z_copies(t, k, way):
        at = pl.ds(k * piece, piece)
        device = (ahead, behind)[way]
        pair = [remote(tokens.at[t, at, :], tokens.at[t, at, :], zs.at[way, t, k], zr.at[t, k], device)]
        if k == 0:
            pair.append(remote(meta.at[t], meta.at[t], ms.at[way, t], mr.at[t], device))
        return pair

    def z_step(off, r, k):
        t, d = my_turns[r][0], hops_at(off, r)
        if d > 0:
            arrived(tokens.at[t, pl.ds(k * piece, piece), :], zr.at[t, k])
            if k == 0:
                arrived(meta.at[t], mr.at[t])
        for way, go in enumerate((d < half_ring, d == 0 or d > half_ring + 1)):
            if go:
                for copy in z_copies(t, k, way):
                    copy.start()

    def z_sent():
        for r in range(turns):
            t, d = my_turns[r]
            for way, go in enumerate((d < half_ring, jnp.logical_or(d == 0, d > half_ring + 1))):
                @pl.when(go)
                def _():
                    for k in range(CHUNKS):
                        for copy in z_copies(t, k, way):
                            copy.wait_send()

    def z_part(part):
        def run(off):
            order = steps_out(off)
            ends = [0]
            for r in range(turns):
                last = max(i for i, step in enumerate(order) if step[1] == r)
                ends.append(max(ends[-1], last + 1))
            for _, r, k in order[ends[part] : ends[part + 1]]:
                z_step(off, r, k)

        for_offset(run)

    slot_row = lax.broadcasted_iota(jnp.int32, (unit, block), 0)
    token_lane = lax.broadcasted_iota(jnp.int32, (unit, block), 1)
    same_half = lax.div(slot_row, CAP) == lax.div(token_lane, rows)
    slot_want = jnp.where(same_half, lax.rem(slot_row, CAP), -2).astype(F32)

    def pack(r):
        t, _ = my_turns[r]
        table = meta[t].astype(F32)
        first = (z * units).astype(F32)
        picks, highs, lows = [], [], []
        for u in range(units):
            got = jnp.full((unit, block), -1.0, F32)
            big = jnp.zeros((unit, block), F32)
            small = jnp.zeros((unit, block), F32)
            for k in range(top):
                hit = table[k : k + 1] == first + float(u)
                got = jnp.where(hit, table[top + k : top + k + 1], got)
                big = jnp.where(hit, table[2 * top + k : 2 * top + k + 1], big)
                small = jnp.where(hit, table[3 * top + k : 3 * top + k + 1], small)
            hit = got == slot_want
            picks.append(jnp.where(hit, 1.0, 0.0))
            highs.append(jnp.where(hit, big, 0.0))
            lows.append(jnp.where(hit, small, 0.0))
        chosen = jnp.concatenate(picks, axis=0).astype(BF16)
        mix[t, 0] = jnp.concatenate(highs, axis=0).T.astype(BF16)
        mix[t, 1] = jnp.concatenate(lows, axis=0).T.astype(BF16)
        for j in range(2):
            at = pl.ds(j * cols, cols)
            out = jnp.dot(chosen, tokens[t, :, at], preferred_element_type=F32)
            packed[t, :, :, at] = out.astype(BF16).reshape(units, unit, cols)
        for i, s in enumerate(plane_steps):
            index, device = plane_peer(s)
            send(
                packed.at[t, index], gathered.at[y, t, me], xs.at[t, i], xr.at[t, me], device
            )
        gathered[y, t, me] = packed[t, me]

    def y_send(r):
        t, _ = my_turns[r]
        for s in plane_steps:
            index, _ = plane_peer(s)
            arrived(gathered.at[y, t, index], xr.at[t, index])
        for i, s in enumerate((1, ny - 1) if ny > 2 else (1,)):
            for j in (i, 1 - i):
                part = gather_half(y, t, j)
                send(part, part, ys.at[2 * i + j, t], yr.at[y, t, j], (ctx, x, y_of(s)))

    def gather_half(at_y, t, j):
        return gathered.at[at_y, t, pl.ds(j * (units // 2), units // 2)]

    def y_forward(r):
        for i, s in enumerate((ny - 1, 1) if ny > 2 else (1,)):
            py = y_of(s)
            t, _ = turn(r, py)
            part = gather_half(py, t, i)
            arrived(part, yr.at[py, t, i])
            if ny > 2:
                send(part, part, ys.at[4 + i, t], yr.at[py, t, 2 + i], (ctx, x, y_of(ny - s)))

    def y_rest(r):
        for i, s in enumerate((ny - 1, 1) if ny > 2 else (1,)):
            py = y_of(s)
            t, _ = turn(r, py)
            arrived(gather_half(py, t, 1 - i), yr.at[py, t, 1 - i])

    def y_last(r):
        if ny > 2:
            py = y_of(2)
            t, _ = turn(r, py)
            for i in range(2):
                arrived(gather_half(py, t, i), yr.at[py, t, 2 + i])

    def d_forward():
        for i, s in enumerate((ny - 1, 1) if ny > 2 else (1,)):
            py = y_of(s)
            part = down_rows(py, i, 2)
            arrived(part, dr.at[py, i])
            if ny > 2:
                send(part, part, ds.at[4 + i], dr.at[py, 2 + i], (ctx, x, y_of(ny - s)))

    def d_last():
        for i, s in enumerate((ny - 1, 1) if ny > 2 else (1,)):
            py = y_of(s)
            arrived(down_rows(py, 1 - i, 2), dr.at[py, 1 - i])
        if ny > 2:
            py = y_of(2)
            for i in range(2):
                arrived(down_rows(py, i, 2), dr.at[py, 2 + i])

    def expert(r, s):
        py = y_of(s)
        t, _ = turn(r, py)
        data = gathered[py, t].reshape(units * unit, half)

        def both(weights):
            low = lax.dot_general(data, weights[:, :half], NT, preferred_element_type=F32)
            high = lax.dot_general(data, weights[:, half:], NT, preferred_element_type=F32)
            low = low.reshape(units, unit, share)[:, :CAP]
            return low + high.reshape(units, unit, share)[:, CAP:]

        gate_act = both(gate_v)
        up_act = both(up_v)
        act = gate_act / (1.0 + jnp.exp(-gate_act)) * up_act
        act = act.reshape(units * CAP, share).astype(BF16)
        place = pl.ds(pl.multiple_of(y * share, share), share)
        if s == 0:
            hidden[t, :, place] = act
        else:
            hidden_out[s - 1, r] = act
            send(
                hidden_out.at[s - 1, r], hidden.at[t, :, place], hs.at[s - 1, r], hr.at[y, t],
                (ctx, x, py),
            )

    if turns == 4:
        z_part(0)
        pack(0)
        z_part(1)
        y_send(0)
        pack(1)
        d_forward()
        z_part(2)
        y_send(1)
        y_forward(0)
        pack(2)
        z_part(3)
        y_send(2)
        y_forward(1)
        pack(3)
        local[0].wait()
        local[1].wait()
        expert(0, 0)
        y_rest(0)
        expert(0, 1)
        y_send(3)
        expert(0, 3)
        y_forward(2)
        y_last(0)
        expert(0, 2)
        expert(1, 0)
        y_rest(1)
        expert(1, 1)
        expert(1, 3)
        y_last(1)
        expert(1, 2)
        y_forward(3)
        expert(2, 0)
        expert(3, 0)
        y_rest(2)
        expert(2, 1)
        expert(2, 3)
        y_last(2)
        expert(2, 2)
        y_rest(3)
        expert(3, 1)
        expert(3, 3)
        y_last(3)
        expert(3, 2)
    else:
        for r in range(turns):
            z_part(r)
        for r in range(turns):
            pack(r)
        d_forward()
        local[0].wait()
        local[1].wait()
        for r in range(turns):
            y_send(r)
        for r in range(turns):
            y_forward(r)
        for r in range(turns):
            y_rest(r)
            y_last(r)
            for s in range(ny):
                expert(r, s)
    d_last()

    def answer(r):
        t, _ = my_turns[r]
        for s in range(1, ny):
            py = y_of(s)
            arrived(hidden.at[t, :, pl.ds(pl.multiple_of(py * share, share), share)], hr.at[py, t])
        data = hidden[t]
        step = half // 4
        for j in range(4):
            low = jnp.dot(data, down_v[:, pl.ds(j * step, step)], preferred_element_type=F32)
            high = jnp.dot(data, down_v[:, pl.ds(half + j * step, step)], preferred_element_type=F32)
            low = low.reshape(units, CAP, step)
            high = high.reshape(units, CAP, step)
            both = jnp.concatenate([low, high], axis=1)
            answers[t, :, :, pl.ds(j * step, step)] = both.astype(BF16)
        for i, s in enumerate(plane_steps):
            index, device = plane_peer(s)
            send(answers.at[t, index], returned.at[t, me], rs.at[t, i], rr.at[t, me], device)
        returned[t, me] = answers[t, me]

    def combine(r):
        t, _ = my_turns[r]
        for s in plane_steps:
            index, _ = plane_peer(s)
            arrived(returned.at[t, index], rr.at[t, index])
        for j in range(2):
            at = pl.ds(j * cols, cols)
            data = returned[t, :, :, at].reshape(units * unit, cols)
            partial[t, :, at] = jnp.dot(
                mix[t, 0], data, preferred_element_type=F32
            ) + jnp.dot(mix[t, 1], data, preferred_element_type=F32)

    def reduce_copy(r, k):
        t, d = my_turns[r]
        at = pl.ds(k * piece, piece)
        onward = lax.div(d, half_ring + 1)
        next_z = lax.rem(z + nz + 2 * onward - 1, nz)
        slot = t + (turns - t) * lax.div(d, nz - 1)
        return remote(
            chain_out.at[t, at, :], chain_in.at[slot, at, :], qs.at[t, k], qr.at[slot, k],
            (next_z * nc + c, x, y),
        )

    def z_reduce(off, r, k):
        t, d = my_turns[r][0], hops_at(off, r)
        at = pl.ds(k * piece, piece)
        total = partial[t, at, :]
        if d not in (half_ring, half_ring + 1):
            arrived(chain_in.at[t, at, :], qr.at[t, k])
            total += chain_in[t, at, :].astype(F32)
        if d == 0:
            arrived(chain_in.at[turns, at, :], qr.at[turns, k])
            total += chain_in[turns, at, :].astype(F32)
            final[at, :] = total.astype(BF16)
        else:
            chain_out[t, at, :] = total.astype(BF16)
            reduce_copy(r, k).start()

    def reduce_sent():
        for r in range(turns):
            @pl.when(my_turns[r][1] > 0)
            def _():
                for k in range(CHUNKS):
                    reduce_copy(r, k).wait_send()

    def reduce_part(starting):
        def run(off):
            for wait, r, k in steps_back(off):
                if (wait < CHUNKS and hops_at(off, r) in (half_ring, half_ring + 1)) == starting:
                    z_reduce(off, r, k)

        for_offset(run)

    def hand_out():
        for h in range(2):
            for py in range(ny):
                place = pl.ds(h * rows + py * own, own)
                send(
                    final.at[place, :], finished.at[h], fs.at[h, py], fr.at[h], (ctx, x, py),
                    when=jnp.logical_and(is_owner, y != py),
                )

    if turns == 4:
        for r in (3, 2, 1, 0):
            answer(r)
        combine(3)
        combine(2)
        reduce_part(True)
        combine(1)
        combine(0)
        reduce_part(False)
    else:
        for r in range(turns - 1, -1, -1):
            answer(r)
        for r in range(turns - 1, -1, -1):
            combine(r)
        reduce_part(True)
        reduce_part(False)
    hand_out()

    @pl.when(is_owner)
    def _():
        for h in range(2):
            place = pl.ds(pl.multiple_of(h * rows + y * own, own), own)
            finished[h] = final[place, :]

    @pl.when(jnp.logical_not(is_owner))
    def _():
        for h in range(2):
            arrived(finished.at[h], fr.at[h])

    for h in range(2):
        out_ref[:, pl.ds(h * half, half)] = (state[h] + finished[h].astype(F32)).astype(BF16)

    z_sent()
    reduce_sent()
    for when, copy in sends:
        if when is None:
            copy.wait_send()
        else:
            @pl.when(when)
            def _():
                copy.wait_send()


def on_device(
    size,
    attention_out,
    output_weight,
    residual,
    norm_gain,
    routed_experts,
    route_weights,
    gate_weight,
    up_weight,
    down_weight,
):
    nz, nc, nx, ny = size
    rows, width = residual.shape
    own, half = rows // ny, width // 2
    share = gate_weight.shape[1]
    top = routed_experts.shape[1]
    units, turns, unit, block = nc * nx, nz // ny, 2 * CAP, 2 * rows
    ids = jnp.concatenate([routed_experts.T, routed_experts.T], axis=1)
    choice = jnp.concatenate([route_weights.T, route_weights.T], axis=1)

    def vmem(*shape, dtype=BF16):
        return pltpu.VMEM(shape, dtype)

    def sems(*shape):
        return pltpu.SemaphoreType.DMA(shape)

    whole = pl.BlockSpec(memory_space=pltpu.VMEM)
    far = pl.BlockSpec(memory_space=pl.ANY)
    return pl.pallas_call(
        functools.partial(kernel, size),
        out_shape=jax.ShapeDtypeStruct((own, width), BF16),
        in_specs=[whole] * 6 + [far] * 3,
        out_specs=whole,
        scratch_shapes=[
            vmem(share, width),
            vmem(share, width),
            vmem(ny * share, width),
            vmem(ny, nx, own, half),
            vmem(nx, ny, own, half),
            vmem(ny, nx, own, half),
            vmem(nx, ny, own, half),
            vmem(nx, own, half),
            vmem(ny, own, half),
            vmem(nx, own, half),
            vmem(ny, own, half),
            vmem(2, own, half, dtype=F32),
            vmem(2, own, half),
            vmem(turns, block, half),
            vmem(turns, 4 * top, block),
            vmem(turns, 2, block, units * unit),
            vmem(turns, units, unit, half),
            vmem(ny, turns, units, unit, half),
            vmem(ny - 1, turns, units * CAP, share),
            vmem(turns, units * CAP, ny * share),
            vmem(turns, units, unit, half),
            vmem(turns, units, unit, half),
            vmem(turns, block, half, dtype=F32),
            vmem(turns + 1, block, half),
            vmem(turns, block, half),
            vmem(block, half),
            vmem(2, own, half),
            sems(4),
            sems(ny), sems(ny), sems(nx), sems(nx), sems(nx), sems(nx), sems(ny), sems(ny),
            sems(2), sems(ny, 2),
            sems(6), sems(ny, 4),
            sems(2, turns, CHUNKS), sems(turns, CHUNKS), sems(2, turns), sems(turns),
            sems(turns, units), sems(turns, units),
            sems(6, turns), sems(ny, turns, 4),
            sems(ny, turns), sems(ny, turns),
            sems(turns, units), sems(turns, units),
            sems(turns, CHUNKS), sems(turns + 1, CHUNKS),
            sems(2, ny), sems(2),
        ],
        compiler_params=pltpu.CompilerParams(
            collective_id=0, has_side_effects=True, vmem_limit_bytes=56 * 1024 * 1024
        ),
    )(
        attention_out, output_weight, residual, norm_gain.reshape(1, -1), ids, choice,
        gate_weight[0], up_weight[0], down_weight[0],
    )


def solution(mesh):
    nc = min(CORES, mesh.shape["ctx"])
    size = (mesh.shape["ctx"] // nc, nc, mesh.shape["tp"], mesh.shape["dp"])
    in_specs = (
        P("ctx", ("tp", "dp")),
        P(("tp", "dp"), None),
        P(("ctx", "tp"), None),
        P(),
        P(("ctx", "tp"), None),
        P(("ctx", "tp"), None),
        P(("ctx", "tp"), "dp", None),
        P(("ctx", "tp"), "dp", None),
        P(("ctx", "tp"), "dp", None),
    )
    out_specs = P(("ctx", "tp", "dp"), None)
    return jax.shard_map(
        functools.partial(on_device, size),
        mesh=mesh, in_specs=in_specs, out_specs=out_specs, check_vma=False,
    )
```

```python
import functools
import jax
import jax.numpy as jnp
from jax import lax
from jax.experimental import pallas as pl
from jax.experimental.pallas import tpu as pltpu
from jax.sharding import PartitionSpec as P

EPSILON = 1e-06
F32 = jnp.float32
BF16 = jnp.bfloat16
MESH = pl.DeviceIdType.MESH
CAP = 8
CORES = 2
CHUNKS = 4
HOP = 3
NT = (((1,), (1,)), ((), ()))


def kernel(
    size,
    attn_ref,
    weight_ref,
    residual_ref,
    gain_ref,
    ids_ref,
    choice_ref,
    gate_ref,
    up_ref,
    down_ref,
    out_ref,
    gate_v,
    up_v,
    down_v,
    part0,
    part1,
    first0,
    first1,
    sum0,
    sum1,
    last0,
    last1,
    state,
    normed,
    tokens,
    meta,
    mix,
    packed,
    gathered,
    hidden_out,
    hidden,
    answers,
    returned,
    partial,
    chain_in,
    chain_out,
    final,
    finished,
    local_sem,
    a0s, a0r, a1s, a1r, b0s, b0r, b1s, b1r,
    ns, nr,
    ds, dr,
    zs, zr, ms, mr,
    xs, xr,
    ys, yr,
    hs, hr,
    rs, rr,
    qs, qr,
    fs, fr,
):
    nz, nc, nx, ny = size
    units = nc * nx
    turns = nz // ny
    half_ring = nz // 2
    ctx, x, y = lax.axis_index("ctx"), lax.axis_index("tp"), lax.axis_index("dp")
    z, c = lax.div(ctx, nc), lax.rem(ctx, nc)
    me = c * nx + x
    own, width = out_ref.shape
    rows = own * ny
    half = width // 2
    share = gate_v.shape[0]
    block = 2 * rows
    piece = block // CHUNKS
    unit = 2 * CAP
    sends = []

    def remote(src, dst, send_sem, recv_sem, device):
        return pltpu.make_async_remote_copy(
            src_ref=src, dst_ref=dst, send_sem=send_sem, recv_sem=recv_sem,
            device_id=device, device_id_type=MESH,
        )

    def send(src, dst, send_sem, recv_sem, device, when=None):
        copy = remote(src, dst, send_sem, recv_sem, device)
        if when is None:
            copy.start()
        else:
            @pl.when(when)
            def _():
                copy.start()
        sends.append((when, copy))

    def arrived(dst, recv_sem):
        remote(dst, dst, local_sem.at[3], recv_sem, ahead).wait_recv()

    def y_of(step):
        return lax.rem(y + step, ny)

    ahead = (lax.rem(z + 1, nz) * nc + c, x, y)
    behind = (lax.rem(z + nz - 1, nz) * nc + c, x, y)
    x_steps = [(0, dx) for dx in range(1, nx)]
    plane_steps = [(dc, dx) for dc in range(nc) for dx in range(nx) if (dc, dx) != (0, 0)]

    def plane_peer(step):
        pc, px = lax.rem(c + step[0], nc), lax.rem(x + step[1], nx)
        return pc * nx + px, (z * nc + pc, px, y)

    peers = [ahead, behind]
    peers += [plane_peer(s)[1] for s in plane_steps]
    peers += [(ctx, x, y_of(s)) for s in range(1, ny)]
    barrier = pltpu.get_barrier_semaphore()
    for peer in peers:
        pl.semaphore_signal(barrier, inc=1, device_id=peer, device_id_type=MESH)

    def down_rows(at_y, part=0, parts=1):
        count = share // parts
        return down_v.at[pl.ds(pl.multiple_of(at_y * share + part * count, count), count)]

    local = [
        pltpu.make_async_copy(gate_ref, gate_v, local_sem.at[0]),
        pltpu.make_async_copy(up_ref, up_v, local_sem.at[1]),
        pltpu.make_async_copy(down_ref, down_rows(y), local_sem.at[2]),
    ]
    for copy in (local[2], local[0], local[1]):
        copy.start()

    attn = attn_ref[...]
    cols = half // 2
    for j in range(2):
        at = pl.ds(j * cols, cols)
        prod = jnp.dot(attn, weight_ref[:, at], preferred_element_type=F32).astype(BF16)
        for px in range(nx):
            for py in range(ny):
                lo = px * rows + py * own
                part0[py, px, :, at] = prod[lo : lo + own]
    pl.semaphore_wait(barrier, len(peers))
    for s in range(1, ny):
        py = y_of(s)
        send(part0.at[py], first0.at[y], a0s.at[py], a0r.at[y], (ctx, x, py))
    for j in range(2):
        at = pl.ds(j * cols, cols)
        prod = jnp.dot(
            attn, weight_ref[:, pl.ds(half + j * cols, cols)], preferred_element_type=F32
        ).astype(BF16)
        for px in range(nx):
            for py in range(ny):
                lo = px * rows + py * own
                part1[px, py, :, at] = prod[lo : lo + own]
    for s in x_steps:
        px = lax.rem(x + s[1], nx)
        send(part1.at[px], first1.at[x], a1s.at[px], a1r.at[x], (ctx, px, y))

    def d_send(second):
        for i, s in enumerate((1, ny - 1) if ny > 2 else (1,)):
            j = 1 - i if second else i
            part = down_rows(y, j, 2)
            send(part, part, ds.at[2 * i + j], dr.at[y, j], (ctx, x, y_of(s)))

    ids = ids_ref[...].astype(F32)
    ids = jnp.concatenate([ids, ids], axis=1)
    top = ids.shape[0]
    experts = nz * units
    expert_row = lax.broadcasted_iota(jnp.int32, (experts, block), 0).astype(F32)
    named = jnp.zeros((experts, block), F32)
    for k in range(top):
        named = jnp.where(ids[k : k + 1] == expert_row, 1.0, named)
    from_row = lax.broadcasted_iota(jnp.int32, (block, block), 0)
    to_row = lax.broadcasted_iota(jnp.int32, (block, block), 1)
    earlier = jnp.where(
        jnp.logical_or(
            from_row < jnp.minimum(to_row, rows),
            jnp.logical_and(from_row < to_row - rows, from_row < rows),
        ),
        1.0,
        0.0,
    )
    earlier = jnp.where(
        jnp.logical_and(to_row >= rows, from_row >= to_row - rows), 0.0, earlier
    )
    count = jnp.dot(named.astype(BF16), earlier.astype(BF16), preferred_element_type=F32)
    slots = jnp.concatenate(
        [
            jnp.sum(jnp.where(ids[k : k + 1] == expert_row, count, 0.0), axis=0, keepdims=True)
            for k in range(top)
        ],
        axis=0,
    )
    choice = jnp.concatenate([choice_ref[...], choice_ref[...]], axis=1)
    probs = choice / jnp.sum(choice, axis=0, keepdims=True)
    high = probs.astype(BF16).astype(F32)
    turn_own = lax.div(z, ny)
    y_own = lax.rem(z, ny)
    routing = jnp.concatenate([ids, slots, high, probs - high], axis=0).astype(BF16)
    is_owner = y == y_own

    @pl.when(is_owner)
    def _():
        meta[turn_own] = routing

    for s in range(1, ny):
        py = y_of(s)
        arrived(first0.at[py], a0r.at[py])
    for px in range(nx):
        total = part0[y, px].astype(F32)
        for s in range(1, ny):
            total += first0[y_of(s), px].astype(F32)
        sum0[px] = total.astype(BF16)
    for s in x_steps:
        px = lax.rem(x + s[1], nx)
        send(sum0.at[px], last0.at[x], b0s.at[px], b0r.at[x], (ctx, px, y))
    for s in x_steps:
        px = lax.rem(x + s[1], nx)
        arrived(first1.at[px], a1r.at[px])
    for py in range(ny):
        total = part1[x, py].astype(F32)
        for s in x_steps:
            total += first1[lax.rem(x + s[1], nx), py].astype(F32)
        sum1[py] = total.astype(BF16)
    for s in range(1, ny):
        py = y_of(s)
        send(sum1.at[py], last1.at[y], b1s.at[py], b1r.at[y], (ctx, x, py))
    mine = pl.ds(pl.multiple_of(y * own, own), own)
    low_sum = sum0[x].astype(F32) + residual_ref[mine, :half].astype(F32)
    high_sum = sum1[y].astype(F32) + residual_ref[mine, half:].astype(F32)
    for s in x_steps:
        px = lax.rem(x + s[1], nx)
        arrived(last0.at[px], b0r.at[px])
        low_sum += last0[px].astype(F32)
    for s in range(1, ny):
        py = y_of(s)
        arrived(last1.at[py], b1r.at[py])
        high_sum += last1[py].astype(F32)
    state[0] = low_sum
    state[1] = high_sum
    square = (
        jnp.sum(low_sum * low_sum, axis=-1, keepdims=True)
        + jnp.sum(high_sum * high_sum, axis=-1, keepdims=True)
    ) / width
    scale = lax.rsqrt(square + EPSILON)
    normed[0] = (low_sum * scale * gain_ref[:, :half]).astype(BF16)
    normed[1] = (high_sum * scale * gain_ref[:, half:]).astype(BF16)

    for h in range(2):
        place = pl.ds(pl.multiple_of(h * rows + y * own, own), own)
        send(
            normed.at[h], tokens.at[turn_own, place, :], ns.at[h], nr.at[y, h],
            (ctx, x, y_own), when=y != y_own,
        )

    @pl.when(is_owner)
    def _():
        for h in range(2):
            place = pl.ds(pl.multiple_of(h * rows + y * own, own), own)
            tokens[turn_own, place, :] = normed[h]
        for s in range(1, ny):
            py = y_of(s)
            for h in range(2):
                place = pl.ds(pl.multiple_of(h * rows + py * own, own), own)
                arrived(tokens.at[turn_own, place, :], nr.at[py, h])

    local[2].wait()
    d_send(False)
    d_send(True)

    tables = {4: ((0, 3, 1, 2), (3, 0, 2, 1)), 2: ((0, 1), (1, 0)), 1: ((0,), (0,))}[turns]

    def turn(r, at_y):
        off = lax.rem(z + ny - at_y, ny)
        near, far = tables[0][r], tables[1][r]
        late = lax.div(2 * off, ny + 1)
        distance = off + ny * (near + (far - near) * late)
        return lax.div(lax.rem(z + nz - distance, nz), ny), distance

    my_turns = [turn(r, y) for r in range(turns)]
    my_off = lax.rem(z + ny - y, ny)

    def hops_at(off, r):
        return off + ny * tables[2 * off // (ny + 1)][r]

    def steps_out(off):
        order = []
        for r in range(turns):
            d = hops_at(off, r)
            order += [(HOP * min(d, nz - d) + k, r, k) for k in range(CHUNKS)]
        return sorted(order)

    def steps_back(off):
        order = []
        for r in range(turns):
            d = hops_at(off, r)
            waited = half_ring - d if d <= half_ring else d - half_ring - 1
            order += [(HOP * waited + k, r, k) for k in range(CHUNKS)]
        return sorted(order)

    def for_offset(run):
        for off in range(ny):
            @pl.when(my_off == off)
            def _():
                run(off)

    def z_copies(t, k, way):
        at = pl.ds(k * piece, piece)
        device = (ahead, behind)[way]
        pair = [remote(tokens.at[t, at, :], tokens.at[t, at, :], zs.at[way, t, k], zr.at[t, k], device)]
        if k == 0:
            pair.append(remote(meta.at[t], meta.at[t], ms.at[way, t], mr.at[t], device))
        return pair

    def z_step(off, r, k):
        t, d = my_turns[r][0], hops_at(off, r)
        if d > 0:
            arrived(tokens.at[t, pl.ds(k * piece, piece), :], zr.at[t, k])
            if k == 0:
                arrived(meta.at[t], mr.at[t])
        for way, go in enumerate((d < half_ring, d == 0 or d > half_ring + 1)):
            if go:
                for copy in z_copies(t, k, way):
                    copy.start()

    def z_sent():
        for r in range(turns):
            t, d = my_turns[r]
            for way, go in enumerate((d < half_ring, jnp.logical_or(d == 0, d > half_ring + 1))):
                @pl.when(go)
                def _():
                    for k in range(CHUNKS):
                        for copy in z_copies(t, k, way):
                            copy.wait_send()

    def z_part(part):
        def run(off):
            order = steps_out(off)
            ends = [0]
            for r in range(turns):
                last = max(i for i, step in enumerate(order) if step[1] == r)
                ends.append(max(ends[-1], last + 1))
            for _, r, k in order[ends[part] : ends[part + 1]]:
                z_step(off, r, k)

        for_offset(run)

    slot_row = lax.broadcasted_iota(jnp.int32, (unit, block), 0)
    token_lane = lax.broadcasted_iota(jnp.int32, (unit, block), 1)
    same_half = lax.div(slot_row, CAP) == lax.div(token_lane, rows)
    slot_want = jnp.where(same_half, lax.rem(slot_row, CAP), -2).astype(F32)

    def routed_here(t, values):
        table = meta[t].astype(F32)
        first = (z * units).astype(F32)
        found = [[] for _ in range(1 + values)]
        for u in range(units):
            got = [jnp.full((unit, block), -1.0, F32)]
            got += [jnp.zeros((unit, block), F32)] * values
            for k in range(top):
                hit = table[k : k + 1] == first + float(u)
                for i in range(1 + values):
                    row = (1 + i) * top + k
                    got[i] = jnp.where(hit, table[row : row + 1], got[i])
            hit = got[0] == slot_want
            for i in range(1 + values):
                found[i].append(jnp.where(hit, 1.0 if i == 0 else got[i], 0.0))
        return [jnp.concatenate(parts, axis=0) for parts in found]

    def weigh(r):
        t, _ = my_turns[r]
        _, big, small = routed_here(t, 2)
        mix[t, 0] = big.T.astype(BF16)
        mix[t, 1] = small.T.astype(BF16)

    def pack(r):
        t, _ = my_turns[r]
        chosen = routed_here(t, 0)[0].astype(BF16)
        for j in range(2):
            at = pl.ds(j * cols, cols)
            out = jnp.dot(chosen, tokens[t, :, at], preferred_element_type=F32)
            packed[t, :, :, at] = out.astype(BF16).reshape(units, unit, cols)
        for i, s in enumerate(plane_steps):
            index, device = plane_peer(s)
            send(
                packed.at[t, index], gathered.at[y, t, me], xs.at[t, i], xr.at[t, me], device
            )
        gathered[y, t, me] = packed[t, me]

    def y_send(r):
        t, _ = my_turns[r]
        for s in plane_steps:
            index, _ = plane_peer(s)
            arrived(gathered.at[y, t, index], xr.at[t, index])
        for i, s in enumerate((1, ny - 1) if ny > 2 else (1,)):
            for j in (i, 1 - i):
                part = gather_half(y, t, j)
                send(part, part, ys.at[2 * i + j, t], yr.at[y, t, j], (ctx, x, y_of(s)))

    def gather_half(at_y, t, j):
        return gathered.at[at_y, t, pl.ds(j * (units // 2), units // 2)]

    def y_forward(r):
        for i, s in enumerate((ny - 1, 1) if ny > 2 else (1,)):
            py = y_of(s)
            t, _ = turn(r, py)
            part = gather_half(py, t, i)
            arrived(part, yr.at[py, t, i])
            if ny > 2:
                send(part, part, ys.at[4 + i, t], yr.at[py, t, 2 + i], (ctx, x, y_of(ny - s)))

    def y_rest(r):
        for i, s in enumerate((ny - 1, 1) if ny > 2 else (1,)):
            py = y_of(s)
            t, _ = turn(r, py)
            arrived(gather_half(py, t, 1 - i), yr.at[py, t, 1 - i])

    def y_last(r):
        if ny > 2:
            py = y_of(2)
            t, _ = turn(r, py)
            for i in range(2):
                arrived(gather_half(py, t, i), yr.at[py, t, 2 + i])

    def d_forward():
        for i, s in enumerate((ny - 1, 1) if ny > 2 else (1,)):
            py = y_of(s)
            part = down_rows(py, i, 2)
            arrived(part, dr.at[py, i])
            if ny > 2:
                send(part, part, ds.at[4 + i], dr.at[py, 2 + i], (ctx, x, y_of(ny - s)))

    def d_last():
        for i, s in enumerate((ny - 1, 1) if ny > 2 else (1,)):
            py = y_of(s)
            arrived(down_rows(py, 1 - i, 2), dr.at[py, 1 - i])
        if ny > 2:
            py = y_of(2)
            for i in range(2):
                arrived(down_rows(py, i, 2), dr.at[py, 2 + i])

    def expert(r, s):
        py = y_of(s)
        t, _ = turn(r, py)
        data = gathered[py, t].reshape(units * unit, half)

        def both(weights):
            low = lax.dot_general(data, weights[:, :half], NT, preferred_element_type=F32)
            high = lax.dot_general(data, weights[:, half:], NT, preferred_element_type=F32)
            low = low.reshape(units, unit, share)[:, :CAP]
            return low + high.reshape(units, unit, share)[:, CAP:]

        gate_act = both(gate_v)
        up_act = both(up_v)
        act = gate_act / (1.0 + jnp.exp(-gate_act)) * up_act
        act = act.reshape(units * CAP, share).astype(BF16)
        place = pl.ds(pl.multiple_of(y * share, share), share)
        if s == 0:
            hidden[t, :, place] = act
        else:
            hidden_out[s - 1, r] = act
            send(
                hidden_out.at[s - 1, r], hidden.at[t, :, place], hs.at[s - 1, r], hr.at[y, t],
                (ctx, x, py),
            )

    if turns == 4:
        z_part(0)
        pack(0)
        z_part(1)
        y_send(0)
        pack(1)
        z_part(2)
        y_send(1)
        y_forward(0)
        pack(2)
        z_part(3)
        y_send(2)
        y_forward(1)
        pack(3)
        local[0].wait()
        local[1].wait()
        expert(0, 0)
        weigh(3)
        weigh(2)
        y_rest(0)
        expert(0, 1)
        y_send(3)
        d_forward()
        expert(0, 3)
        y_forward(2)
        y_last(0)
        expert(0, 2)
        expert(1, 0)
        y_rest(1)
        expert(1, 1)
        expert(1, 3)
        y_last(1)
        expert(1, 2)
        y_forward(3)
        weigh(1)
        weigh(0)
        expert(2, 0)
        expert(3, 0)
        y_rest(2)
        expert(2, 1)
        expert(2, 3)
        y_last(2)
        expert(2, 2)
        y_rest(3)
        expert(3, 1)
        expert(3, 3)
        y_last(3)
        expert(3, 2)
    else:
        for r in range(turns):
            z_part(r)
        for r in range(turns):
            pack(r)
            weigh(r)
        d_forward()
        local[0].wait()
        local[1].wait()
        for r in range(turns):
            y_send(r)
        for r in range(turns):
            y_forward(r)
        for r in range(turns):
            y_rest(r)
            y_last(r)
            for s in range(ny):
                expert(r, s)
    d_last()

    def answer(r):
        t, _ = my_turns[r]
        for s in range(1, ny):
            py = y_of(s)
            arrived(hidden.at[t, :, pl.ds(pl.multiple_of(py * share, share), share)], hr.at[py, t])
        data = hidden[t]
        step = half // 4
        for j in range(4):
            low = jnp.dot(data, down_v[:, pl.ds(j * step, step)], preferred_element_type=F32)
            high = jnp.dot(data, down_v[:, pl.ds(half + j * step, step)], preferred_element_type=F32)
            low = low.reshape(units, CAP, step)
            high = high.reshape(units, CAP, step)
            both = jnp.concatenate([low, high], axis=1)
            answers[t, :, :, pl.ds(j * step, step)] = both.astype(BF16)
        for i, s in enumerate(plane_steps):
            index, device = plane_peer(s)
            send(answers.at[t, index], returned.at[t, me], rs.at[t, i], rr.at[t, me], device)
        returned[t, me] = answers[t, me]

    def combine(r):
        t, _ = my_turns[r]
        for s in plane_steps:
            index, _ = plane_peer(s)
            arrived(returned.at[t, index], rr.at[t, index])
        for j in range(2):
            at = pl.ds(j * cols, cols)
            data = returned[t, :, :, at].reshape(units * unit, cols)
            partial[t, :, at] = jnp.dot(
                mix[t, 0], data, preferred_element_type=F32
            ) + jnp.dot(mix[t, 1], data, preferred_element_type=F32)

    def reduce_copy(r, k):
        t, d = my_turns[r]
        at = pl.ds(k * piece, piece)
        onward = lax.div(d, half_ring + 1)
        next_z = lax.rem(z + nz + 2 * onward - 1, nz)
        slot = t + (turns - t) * lax.div(d, nz - 1)
        return remote(
            chain_out.at[t, at, :], chain_in.at[slot, at, :], qs.at[t, k], qr.at[slot, k],
            (next_z * nc + c, x, y),
        )

    def z_reduce(off, r, k):
        t, d = my_turns[r][0], hops_at(off, r)
        at = pl.ds(k * piece, piece)
        total = partial[t, at, :]
        if d not in (half_ring, half_ring + 1):
            arrived(chain_in.at[t, at, :], qr.at[t, k])
            total += chain_in[t, at, :].astype(F32)
        if d == 0:
            arrived(chain_in.at[turns, at, :], qr.at[turns, k])
            total += chain_in[turns, at, :].astype(F32)
            final[at, :] = total.astype(BF16)
            for row in range(k * piece, (k + 1) * piece, own):
                h, py = row // rows, row % rows // own

                @pl.when(y != py)
                def _():
                    hand_copy(h, py).start()
        else:
            chain_out[t, at, :] = total.astype(BF16)
            reduce_copy(r, k).start()

    def reduce_sent():
        for r in range(turns):
            @pl.when(my_turns[r][1] > 0)
            def _():
                for k in range(CHUNKS):
                    reduce_copy(r, k).wait_send()

    def reduce_part(part):
        def run(off):
            for wait, r, k in steps_back(off):
                begins = hops_at(off, r) in (half_ring, half_ring + 1)
                if part == (0 if begins else 1 if turns == 4 and wait < 2 * HOP + 1 and r > 1 else 2):
                    z_reduce(off, r, k)

        for_offset(run)

    def hand_copy(h, py):
        place = pl.ds(h * rows + py * own, own)
        return remote(final.at[place, :], finished.at[h], fs.at[h, py], fr.at[h], (ctx, x, py))

    def handed_out():
        for py in range(ny):
            @pl.when(jnp.logical_and(is_owner, y != py))
            def _():
                for h in range(2):
                    hand_copy(h, py).wait_send()

    if turns == 4:
        answer(3)
        answer(2)
        combine(3)
        reduce_part(0)
        combine(2)
        answer(1)
        answer(0)
        reduce_part(1)
        combine(1)
        combine(0)
        reduce_part(2)
    else:
        for r in range(turns - 1, -1, -1):
            answer(r)
        for r in range(turns - 1, -1, -1):
            combine(r)
        reduce_part(0)
        reduce_part(2)

    @pl.when(is_owner)
    def _():
        for h in range(2):
            place = pl.ds(pl.multiple_of(h * rows + y * own, own), own)
            finished[h] = final[place, :]

    @pl.when(jnp.logical_not(is_owner))
    def _():
        for h in range(2):
            arrived(finished.at[h], fr.at[h])

    for h in range(2):
        out_ref[:, pl.ds(h * half, half)] = (state[h] + finished[h].astype(F32)).astype(BF16)

    z_sent()
    reduce_sent()
    handed_out()
    for when, copy in sends:
        if when is None:
            copy.wait_send()
        else:
            @pl.when(when)
            def _():
                copy.wait_send()


def on_device(
    size,
    attention_out,
    output_weight,
    residual,
    norm_gain,
    routed_experts,
    route_weights,
    gate_weight,
    up_weight,
    down_weight,
):
    nz, nc, nx, ny = size
    rows, width = residual.shape
    own, half = rows // ny, width // 2
    share = gate_weight.shape[1]
    top = routed_experts.shape[1]
    units, turns, unit, block = nc * nx, nz // ny, 2 * CAP, 2 * rows
    ids, choice = routed_experts.T, route_weights.T

    def vmem(*shape, dtype=BF16):
        return pltpu.VMEM(shape, dtype)

    def sems(*shape):
        return pltpu.SemaphoreType.DMA(shape)

    whole = pl.BlockSpec(memory_space=pltpu.VMEM)
    far = pl.BlockSpec(memory_space=pl.ANY)
    return pl.pallas_call(
        functools.partial(kernel, size),
        out_shape=jax.ShapeDtypeStruct((own, width), BF16),
        in_specs=[whole] * 6 + [far] * 3,
        out_specs=whole,
        scratch_shapes=[
            vmem(share, width),
            vmem(share, width),
            vmem(ny * share, width),
            vmem(ny, nx, own, half),
            vmem(nx, ny, own, half),
            vmem(ny, nx, own, half),
            vmem(nx, ny, own, half),
            vmem(nx, own, half),
            vmem(ny, own, half),
            vmem(nx, own, half),
            vmem(ny, own, half),
            vmem(2, own, half, dtype=F32),
            vmem(2, own, half),
            vmem(turns, block, half),
            vmem(turns, 4 * top, block),
            vmem(turns, 2, block, units * unit),
            vmem(turns, units, unit, half),
            vmem(ny, turns, units, unit, half),
            vmem(ny - 1, turns, units * CAP, share),
            vmem(turns, units * CAP, ny * share),
            vmem(turns, units, unit, half),
            vmem(turns, units, unit, half),
            vmem(turns, block, half, dtype=F32),
            vmem(turns + 1, block, half),
            vmem(turns, block, half),
            vmem(block, half),
            vmem(2, own, half),
            sems(4),
            sems(ny), sems(ny), sems(nx), sems(nx), sems(nx), sems(nx), sems(ny), sems(ny),
            sems(2), sems(ny, 2),
            sems(6), sems(ny, 4),
            sems(2, turns, CHUNKS), sems(turns, CHUNKS), sems(2, turns), sems(turns),
            sems(turns, units), sems(turns, units),
            sems(6, turns), sems(ny, turns, 4),
            sems(ny, turns), sems(ny, turns),
            sems(turns, units), sems(turns, units),
            sems(turns, CHUNKS), sems(turns + 1, CHUNKS),
            sems(2, ny), sems(2),
        ],
        compiler_params=pltpu.CompilerParams(
            collective_id=0, has_side_effects=True, vmem_limit_bytes=56 * 1024 * 1024
        ),
    )(
        attention_out, output_weight, residual, norm_gain.reshape(1, -1), ids, choice,
        gate_weight[0], up_weight[0], down_weight[0],
    )


def solution(mesh):
    nc = min(CORES, mesh.shape["ctx"])
    size = (mesh.shape["ctx"] // nc, nc, mesh.shape["tp"], mesh.shape["dp"])
    in_specs = (
        P("ctx", ("tp", "dp")),
        P(("tp", "dp"), None),
        P(("ctx", "tp"), None),
        P(),
        P(("ctx", "tp"), None),
        P(("ctx", "tp"), None),
        P(("ctx", "tp"), "dp", None),
        P(("ctx", "tp"), "dp", None),
        P(("ctx", "tp"), "dp", None),
    )
    out_specs = P(("ctx", "tp", "dp"), None)
    return jax.shard_map(
        functools.partial(on_device, size),
        mesh=mesh, in_specs=in_specs, out_specs=out_specs, check_vma=False,
    )
```
